32 devices in a mesh: expert: 8 (over z, core), fsdp: 4 (over y, x).
Axes of the slice: x: 2, y: 2, z: 4, core: 2. Of those that a mesh axis runs over, the one named last changes fastest.
Arguments:
- tokens: bfloat16 [16384, 1024], P(('expert', 'fsdp')), may hold values from -6 to 6
- norm_one: bfloat16 [1024], P('fsdp'), may hold values from 0.25 to 1.75
- query_weight: bfloat16 [1024, 1024], P('fsdp'), may hold values from -0.25 to 0.25
- key_projection_matrix: bfloat16 [1024, 512], P('fsdp'), may hold values from -0.1875 to 0.1875
- value_projection_matrix: bfloat16 [1024, 512], P('fsdp'), may hold values from -0.1875 to 0.1875
- out_weight: bfloat16 [1024, 1024], P('fsdp'), may hold values from -0.5 to 0.5
- norm_two: bfloat16 [1024], P('fsdp'), may hold values from 0.25 to 1.75
- router_weight: bfloat16 [1024, 32], P('fsdp'), may hold values from -0.09375 to 0.09375
- gate_weight: bfloat16 [32, 1024, 512], P('expert'), may hold values from -0.1875 to 0.1875
- up_weight: bfloat16 [32, 1024, 512], P('expert'), may hold values from -0.1875 to 0.1875
- down_weight: bfloat16 [32, 512, 1024], P('expert'), may hold values from -0.75 to 0.75
- routes: int32 [16384, 8], P(('expert', 'fsdp')), may hold values from 0 to 31, all different within a row; in each aligned block of 512 rows (0 to 511, 512 to 1023, ...) at most 192 rows name the same one
- out_grad: bfloat16 [16384, 1024], P(('expert', 'fsdp')), may hold values from -6 to 6
Outputs:
- block_out: bfloat16 [16384, 1024], P(('expert', 'fsdp'))
- input_grad: float32 [16384, 1024], P(('expert', 'fsdp'))
- norm_one_grad: float32 [1024], P('fsdp')
- query_grad: float32 [1024, 1024], P('fsdp')
- key_grad: float32 [1024, 512], P('fsdp')
- value_grad: float32 [1024, 512], P('fsdp')
- out_proj_grad: float32 [1024, 1024], P('fsdp')
- norm_two_grad: float32 [1024], P('fsdp')
- router_grad: float32 [1024, 32], P('fsdp')
- gate_grad: float32 [32, 1024, 512], P('expert')
- up_grad: float32 [32, 1024, 512], P('expert')
- down_grad: float32 [32, 512, 1024], P('expert')
The draws below stay inside these ranges and needn't reach their ends.
Inputs may be any that keep to these rules, and one draw needn't show every extreme that they name: `routes`: each row names 8 different experts. Within the 512 rows of one device (aligned blocks) no expert is named by more than 192 rows, and in every draw some expert is named by exactly 192 rows of some block.
All inputs are finite; a program needn't handle non-finite values.
Results may differ from the reference program's by a relative error of at most 0.023.
Values may be sent and summed in bfloat16 or wider, within the bound.
A program may use at most 320 MiB of HBM per device.

```python
import math
import jax
import jax.numpy as jnp
import numpy as np
from jax import lax

MODEL_WIDTH = 1024
QUERY_HEADS = 16
KEY_VALUE_HEADS = 8
HEAD_WIDTH = 64
FF = 512
EXPERTS = 32
TOPK = 8
TOKENS_PER_SHARD = 512
CAP = 192
TOKENS = 16384


def shard_levels(key, shape, cuts, low, largest):
    level = 1.0
    for position, blocks in cuts:
        draws = jax.random.uniform(jax.random.fold_in(jax.random.fold_in(key, 6), position), (blocks,), jnp.float32, low / len(cuts), largest / len(cuts))
        level = level * jnp.repeat(jnp.exp(draws), shape[position] // blocks).reshape((-1,) + (1,) * (len(shape) - 1 - position))
    return level


def shared_out(rng, own, number, rows, count, top, limit, lean):
    ranking = jax.random.permutation(rng, count)
    packed, common = portions_of(count, rows * top, limit, lean, True), portions_of(count, rows * top, limit, lean, False)
    places = jnp.arange(count)

    def named(lengths, offset_by):
        used = int((lengths > 0).sum())
        fixed = max(1, used // 4)
        passed = fixed + (places - fixed + offset_by * (used - fixed)) % max(1, count - fixed)
        return jnp.zeros((count,), jnp.int32).at[ranking[jnp.where(places < fixed, places, passed)]].set(jnp.asarray(lengths, jnp.int32))

    lengths = jnp.where(number % 4 == 0, named(packed, number // 4), named(common, number - number // 4 - 1))
    mixed = jax.random.permutation(jax.random.fold_in(own, 3), count)
    donor, receiver = mixed[0:count // 2 * 2:2], mixed[1:count // 2 * 2:2]
    margin = jnp.minimum(lengths[donor] - 1, limit - lengths[receiver]) // 2
    margin = jnp.where((donor == ranking[0]) | (receiver == ranking[0]) | (lengths[receiver] == 0), 0, jnp.maximum(margin, 0))
    passed = jax.random.randint(jax.random.fold_in(own, 4), (count // 2,), 0, 1 << 20) % (margin + 1)
    lengths = lengths.at[donor].add(-passed).at[receiver].add(passed)
    labels = jnp.searchsorted(jnp.cumsum(lengths), jnp.arange(rows * top), side="right").astype(jnp.int32)
    table = labels.reshape(top, rows).T
    table = table[jax.random.permutation(jax.random.fold_in(own, 1), rows)]
    offset_by = jax.random.randint(jax.random.fold_in(own, 2), (rows, 1), 0, top)
    return jnp.take_along_axis(table, (jnp.arange(top)[None, :] + offset_by) % top, axis=1)


def portions_of(amount, total, bound, slope, full):
    portions = [(1 << 20) // math.isqrt(rank ** slope) + 1 for rank in range(1, amount + 1)]
    largest = bound if full else min(bound, max(-(-total // amount), total * portions[0] // sum(portions)))
    least = 1 if total - largest >= amount - 1 else 0
    given, surplus = [largest] + [least] * (amount - 1), total - largest - least * (amount - 1)
    while surplus > 0:
        movable = [i for i in range(1, amount) if given[i] < largest] or [i for i in range(1, amount) if given[i] < bound]
        mass, remaining = sum([portions[i] for i in movable]), surplus
        for i in movable:
            more = min(bound - given[i], max(1, remaining * portions[i] // mass), surplus)
            given[i] = given[i] + more
            surplus = surplus - more
    return np.array(given)


def scatter_about(key, extent, deviation, reach, shards=(), kind=jnp.bfloat16):
    drawn = deviation * jax.random.normal(key, extent, jnp.float32)
    if shards:
        drawn = drawn * shard_levels(key, extent, shards, -0.22, 0.18)
    return jnp.clip(drawn, -reach, reach).astype(kind)


def setup_inputs(seed: int = 0) -> dict:
    key_of = jax.random.split(jax.random.key(seed), 14)
    tokens = scatter_about(key_of[0], (TOKENS, MODEL_WIDTH), 1.0, 6.0, ((0, 32),))
    norm_one = jnp.clip(1.0 + 0.15 * jax.random.normal(key_of[1], (MODEL_WIDTH,), jnp.float32), 0.25, 1.75).astype(jnp.bfloat16)
    query_weight = scatter_about(key_of[2], (MODEL_WIDTH, QUERY_HEADS * HEAD_WIDTH), (MODEL_WIDTH // 2) ** -0.5, 0.25, ((0, 4),))
    key_projection_matrix = scatter_about(key_of[3], (MODEL_WIDTH, KEY_VALUE_HEADS * HEAD_WIDTH), MODEL_WIDTH ** -0.5, 0.1875, ((0, 4),))
    value_projection_matrix = scatter_about(key_of[4], (MODEL_WIDTH, KEY_VALUE_HEADS * HEAD_WIDTH), MODEL_WIDTH ** -0.5, 0.1875, ((0, 4),))
    out_weight = scatter_about(key_of[5], (QUERY_HEADS * HEAD_WIDTH, MODEL_WIDTH), (QUERY_HEADS * HEAD_WIDTH // 8) ** -0.5, 0.5, ((0, 4),))
    norm_two = jnp.clip(1.0 + 0.15 * jax.random.normal(key_of[6], (MODEL_WIDTH,), jnp.float32), 0.25, 1.75).astype(jnp.bfloat16)
    router_weight = scatter_about(key_of[7], (MODEL_WIDTH, EXPERTS), (4 * MODEL_WIDTH) ** -0.5, 0.09375, ((0, 4),))
    gate_weight = scatter_about(key_of[8], (EXPERTS, MODEL_WIDTH, FF), MODEL_WIDTH ** -0.5, 0.1875, ((0, 8),))
    up_weight = scatter_about(key_of[9], (EXPERTS, MODEL_WIDTH, FF), MODEL_WIDTH ** -0.5, 0.1875, ((0, 8),))
    down_weight = scatter_about(key_of[10], (EXPERTS, FF, MODEL_WIDTH), (FF // 8) ** -0.5, 0.75, ((0, 8),))
    routes_keys = jax.random.split(jax.random.fold_in(key_of[11], 1), TOKENS // TOKENS_PER_SHARD)
    routes_turns = jax.random.permutation(jax.random.fold_in(key_of[11], 3), TOKENS // TOKENS_PER_SHARD)
    routes = jax.vmap(lambda own, number: shared_out(jax.random.fold_in(key_of[11], 2), own, number, TOKENS_PER_SHARD, EXPERTS, TOPK, CAP, 1))(routes_keys, routes_turns).reshape((TOKENS, TOPK))
    out_grad = scatter_about(key_of[12], (TOKENS, MODEL_WIDTH), 1.0, 6.0, ((0, 32),))
    return dict(tokens=tokens, norm_one=norm_one, query_weight=query_weight, key_projection_matrix=key_projection_matrix, value_projection_matrix=value_projection_matrix, out_weight=out_weight, norm_two=norm_two, router_weight=router_weight, gate_weight=gate_weight, up_weight=up_weight, down_weight=down_weight, routes=routes, out_grad=out_grad)


EPSILON = 1e-05
THETA = 10000.0
NEGATIVE = -1e+30
HIGH_PRECISION = lax.Precision.HIGHEST

@jax.custom_vjp
def reduced_input(v):
    return lax.optimization_barrier(v.astype(jnp.bfloat16)).astype(jnp.float32)

@jax.custom_vjp
def reduced_input_gradient(v):
    return v

def low_keep(v):
    return (reduced_input(v), None)

def low_pass(kept, grad):
    return (grad,)

def back_keep(v):
    return (v, None)

def back_low(kept, grad):
    return (reduced_input(grad),)
reduced_input.defvjp(low_keep, low_pass)
reduced_input_gradient.defvjp(back_keep, back_low)

def rms_scale(values, gain):
    return values * lax.rsqrt(lax.optimization_barrier(jnp.mean(values * values, axis=-1, keepdims=True)) + EPSILON) * gain

def rope_tables(length, head_size):
    half_size = head_size // 2
    freqs = jnp.power(THETA, -2.0 * jnp.arange(half_size).astype(jnp.float32) / head_size)
    angles = jnp.arange(length).astype(jnp.float32)[:, None] * freqs[None, :]
    return (jnp.cos(angles), jnp.sin(angles))

def apply_rotation_heads(values, cosine_table, sine_table, direction):
    half_size = values.shape[-1] // 2
    lead_half = values[..., :half_size]
    tail_half = values[..., half_size:]
    cos_part = cosine_table[:, None, :]
    sin_part = sine_table[:, None, :] * direction
    return jnp.concatenate([lead_half * cos_part - tail_half * sin_part, tail_half * cos_part + lead_half * sin_part], axis=-1)

def silu_fn(values):
    return values * jax.nn.sigmoid(values)

def attend(pieces):
    query_rotated, key_rotated, value_per_head = pieces
    length = query_rotated.shape[0]
    attention_scores = reduced_input_gradient(jnp.einsum('mhwo,pho->hwmp', query_rotated, key_rotated, precision=HIGH_PRECISION) * HEAD_WIDTH ** (-0.5))
    causal = jnp.arange(length)[:, None] >= jnp.arange(length)[None, :]
    masked = jnp.where(causal, attention_scores, NEGATIVE)
    row_top = lax.optimization_barrier(jnp.max(masked, axis=-1, keepdims=True))
    expo = jnp.exp(masked - row_top)
    attention_probability = reduced_input(expo / lax.optimization_barrier(jnp.sum(expo, axis=-1, keepdims=True)))
    return jnp.einsum('nfea,anm->enfm', attention_probability, value_per_head, precision=HIGH_PRECISION)

def reference(tokens, norm_one, query_weight, key_projection_matrix, value_projection_matrix, out_weight, norm_two, router_weight, gate_weight, up_weight, down_weight, routes, out_grad):
    block_list = TOKENS // TOKENS_PER_SHARD
    pairs = TOKENS * TOPK
    flat_route = routes.reshape(-1).astype(jnp.int32)
    pick = (flat_route.reshape(block_list, TOKENS_PER_SHARD * TOPK, 1) == jnp.arange(EXPERTS).astype(jnp.int32)[None, None, :]).astype(jnp.int32)
    running = jnp.cumsum(pick, axis=1) - 1
    slot_index = lax.optimization_barrier(jnp.sum(running * pick, axis=2)).reshape(-1).astype(jnp.int32)
    block_index = (jnp.arange(pairs) // (TOKENS_PER_SHARD * TOPK)).astype(jnp.int32)
    column = block_index * CAP + slot_index
    pair_ids = jnp.arange(pairs).astype(jnp.int32)
    row_table = jnp.full((EXPERTS, block_list * CAP), TOKENS, jnp.int32).at[flat_route, column].set(pair_ids // TOPK)
    pair_table = jnp.full((EXPERTS, block_list * CAP), pairs, jnp.int32).at[flat_route, column].set(pair_ids)
    route_pick = (routes[:, :, None] == jnp.arange(EXPERTS).astype(jnp.int32)[None, None, :]).astype(jnp.float32)
    query_group_width = QUERY_HEADS // KEY_VALUE_HEADS

    def forward(x_float, gain_first, query_w, key_w, value_w, out_w, gain_second, router_w, gate_w, up_w, down_w):
        normed_one = rms_scale(x_float, gain_first)
        normed_low = reduced_input(normed_one)
        query_pre = reduced_input_gradient(jnp.dot(normed_low, query_w, precision=HIGH_PRECISION))
        key_before_rotation = reduced_input_gradient(jnp.dot(normed_low, key_w, precision=HIGH_PRECISION))
        value_every_head = reduced_input_gradient(reduced_input(jnp.dot(normed_low, value_w, precision=HIGH_PRECISION)))
        cosine_table, sine_table = rope_tables(TOKENS_PER_SHARD, HEAD_WIDTH)
        query_rotated = reduced_input(apply_rotation_heads(query_pre.reshape(block_list, TOKENS_PER_SHARD, QUERY_HEADS, HEAD_WIDTH), cosine_table, sine_table, 1.0))
        query_rotated = query_rotated.reshape(block_list, TOKENS_PER_SHARD, KEY_VALUE_HEADS, query_group_width, HEAD_WIDTH)
        key_rotated = reduced_input(apply_rotation_heads(key_before_rotation.reshape(block_list, TOKENS_PER_SHARD, KEY_VALUE_HEADS, HEAD_WIDTH), cosine_table, sine_table, 1.0))
        value_per_head = value_every_head.reshape(block_list, TOKENS_PER_SHARD, KEY_VALUE_HEADS, HEAD_WIDTH)
        attn_heads = lax.map(jax.checkpoint(attend), (query_rotated, key_rotated, value_per_head))
        attn_low = reduced_input_gradient(reduced_input(attn_heads.reshape(TOKENS, QUERY_HEADS * HEAD_WIDTH)))
        attn_proj = reduced_input_gradient(jnp.dot(attn_low, out_w, precision=HIGH_PRECISION))
        resid_one = x_float + attn_proj
        moe_input = reduced_input(rms_scale(resid_one, gain_second))
        logits = jnp.dot(moe_input, router_w, precision=HIGH_PRECISION)
        chosen = lax.optimization_barrier(jnp.sum(route_pick * logits[:, None, :], axis=-1))
        chosen_top = lax.optimization_barrier(jnp.max(chosen, axis=-1, keepdims=True))
        chosen_exp = jnp.exp(chosen - chosen_top)
        gates = chosen_exp / lax.optimization_barrier(jnp.sum(chosen_exp, axis=-1, keepdims=True))
        gate_flat = jnp.concatenate([gates.reshape(-1), jnp.zeros((1,), gates.dtype)])
        input_pad = jnp.concatenate([moe_input, jnp.zeros((1, MODEL_WIDTH), moe_input.dtype)], axis=0)

        def expert_step(total, pieces):
            row_index, pair_index, gate_one, up_one, down_one = pieces
            expert_rows = reduced_input_gradient(input_pad[row_index])
            gate_pre = reduced_input_gradient(jnp.dot(expert_rows, gate_one, precision=HIGH_PRECISION))
            up_pre = reduced_input_gradient(jnp.dot(expert_rows, up_one, precision=HIGH_PRECISION))
            hidden = reduced_input(silu_fn(gate_pre) * up_pre)
            expert_out = reduced_input_gradient(reduced_input(jnp.dot(hidden, down_one, precision=HIGH_PRECISION)))
            total = total.at[row_index].add(gate_flat[pair_index][:, None] * expert_out)
            return (total, None)
        moe_total, _ = lax.scan(jax.checkpoint(expert_step), jnp.zeros((TOKENS + 1, MODEL_WIDTH), x_float.dtype), (row_table, pair_table, gate_w, up_w, down_w))
        return resid_one + moe_total[:TOKENS]
    floats = (tokens.astype(jnp.float32), norm_one.astype(jnp.float32), query_weight.astype(jnp.float32), key_projection_matrix.astype(jnp.float32), value_projection_matrix.astype(jnp.float32), out_weight.astype(jnp.float32), norm_two.astype(jnp.float32), router_weight.astype(jnp.float32), gate_weight.astype(jnp.float32), up_weight.astype(jnp.float32), down_weight.astype(jnp.float32))
    block_value, pullback = jax.vjp(forward, *floats)
    grads = pullback(out_grad.astype(jnp.float32))
    return (block_value.astype(jnp.bfloat16), grads[0], grads[1], grads[2], grads[3], grads[4], grads[5], grads[6], grads[7], grads[8], grads[9], grads[10])
```

```python
import jax
import jax.numpy as jnp
from jax import lax
from jax.sharding import PartitionSpec as P

MODEL_WIDTH = 1024
QUERY_HEADS = 16
KEY_VALUE_HEADS = 8
HEAD_WIDTH = 64
EXPERTS = 32
TOPK = 8
CAP = 192


EPSILON = 1e-05
THETA = 10000.0
NEGATIVE = -1e30
HIGH_PRECISION = lax.Precision.HIGHEST


def rms_scale(values, gain):
    return values * lax.rsqrt(jnp.mean(values * values, axis=-1, keepdims=True) + EPSILON) * gain


def rope_tables(length, head_size):
    half_size = head_size // 2
    freqs = jnp.power(THETA, -2.0 * jnp.arange(half_size).astype(jnp.float32) / head_size)
    angles = jnp.arange(length).astype(jnp.float32)[:, None] * freqs[None, :]
    return (jnp.cos(angles), jnp.sin(angles))


def apply_rotation_heads(values, cosine_table, sine_table, direction):
    half_size = values.shape[-1] // 2
    lead_half = values[..., :half_size]
    tail_half = values[..., half_size:]
    cos_part = cosine_table[:, None, :]
    sin_part = sine_table[:, None, :] * direction
    return jnp.concatenate(
        [lead_half * cos_part - tail_half * sin_part, tail_half * cos_part + lead_half * sin_part],
        axis=-1,
    )


def inner_rows(left_mat, right_mat):
    return lax.dot_general(
        left_mat, right_mat, (((0,), (0,)), ((), ())), preferred_element_type=jnp.float32
    )


def outer_cols(left_mat, right_mat):
    return lax.dot_general(
        left_mat, right_mat, (((1,), (1,)), ((), ())), preferred_element_type=jnp.float32
    )


def masked_scores(query_rotated, key_rotated):
    length = query_rotated.shape[0]
    attention_scores = jnp.einsum(
        "mhwo,pho->hwmp", query_rotated, key_rotated, preferred_element_type=jnp.float32
    ) * HEAD_WIDTH ** (-0.5)
    causal = jnp.arange(length)[:, None] >= jnp.arange(length)[None, :]
    return jnp.where(causal, attention_scores, NEGATIVE)


def dense_gates(rows, router_full, routes):
    logits = jnp.dot(rows, router_full, preferred_element_type=jnp.float32)
    named = jnp.any(routes[..., None] == jnp.arange(EXPERTS), axis=-2)
    top = jnp.max(jnp.where(named, logits, -jnp.inf), axis=-1, keepdims=True)
    powers = jnp.where(named, jnp.exp(jnp.where(named, logits - top, 0.0)), 0.0)
    return powers / jnp.sum(powers, axis=-1, keepdims=True)


def ring_gather(block, n_expert):
    me = lax.axis_index("expert")
    chips = n_expert // 2
    chip, core = me // 2, me % 2
    step_on = [(i, (i + 2) % n_expert) for i in range(n_expert)]
    held = [block]
    for _ in range(chips - 1):
        held.append(lax.ppermute(held[-1], "expert", step_on))
    swap = [(i, i ^ 1) for i in range(n_expert)]
    gathered = jnp.zeros((chips, 2) + block.shape, block.dtype)
    for k, part in enumerate(held):
        other = lax.ppermute(part, "expert", swap)
        source = (chip - k + chips) % chips
        both = jnp.where(core == 0, jnp.stack([part, other]), jnp.stack([other, part]))
        gathered = lax.dynamic_update_index_in_dim(gathered, both, source, 0)
    return gathered.reshape((n_expert,) + block.shape)


def butterfly_sum(block, bits):
    size = lax.axis_size("fsdp")
    me = lax.axis_index("fsdp")
    width = block.shape[-1]
    current = block.reshape(-1, width)
    for bit in bits:
        side = (me >> bit) & 1
        halves = current.reshape(2, -1, width)
        keep = lax.dynamic_index_in_dim(halves, side, 0, keepdims=False)
        send = lax.dynamic_index_in_dim(halves, 1 - side, 0, keepdims=False)
        got = lax.ppermute(send, "fsdp", [(i, i ^ (1 << bit)) for i in range(size)])
        current = (keep.astype(jnp.float32) + got.astype(jnp.float32)).astype(jnp.bfloat16)
    for bit in reversed(bits):
        side = (me >> bit) & 1
        got = lax.ppermute(current, "fsdp", [(i, i ^ (1 << bit)) for i in range(size)])
        current = jnp.where(
            side == 0, jnp.concatenate([current, got]), jnp.concatenate([got, current])
        )
    return current.reshape(block.shape)


def fsdp_sum(block):
    size = lax.axis_size("fsdp")
    if size & (size - 1):
        return lax.psum(block, "fsdp").astype(jnp.float32)
    bits = list(range(size.bit_length() - 1))
    half = block.shape[0] // 2
    first = butterfly_sum(block[:half], bits)
    second = butterfly_sum(block[half:], bits[::-1])
    return jnp.concatenate([first, second]).astype(jnp.float32)


def reduce_pack(parts, n_expert):
    width = sum(part.shape[1] for part in parts)
    pad = jnp.zeros((parts[0].shape[0], -width % 128), jnp.bfloat16)
    packed = jnp.concatenate([part.astype(jnp.bfloat16) for part in parts] + [pad], axis=1)
    packed = lax.psum_scatter(packed, "fsdp", scatter_dimension=0, tiled=True)
    return lax.psum(packed, "expert").astype(jnp.float32)


def on_device(
    tokens,
    norm_one,
    query_weight,
    key_projection_matrix,
    value_projection_matrix,
    out_weight,
    norm_two,
    router_weight,
    gate_weight,
    up_weight,
    down_weight,
    routes,
    out_grad,
):
    n_expert = lax.axis_size("expert")
    token_rows = tokens.shape[0]
    exp_local = gate_weight.shape[0]
    query_group_width = QUERY_HEADS // KEY_VALUE_HEADS
    kv_width = KEY_VALUE_HEADS * HEAD_WIDTH
    shard_rows = query_weight.shape[0]
    first_pack = jnp.concatenate(
        [
            query_weight,
            key_projection_matrix,
            value_projection_matrix,
            router_weight,
            norm_one[:, None],
            norm_two[:, None],
            jnp.zeros((shard_rows, 128 - EXPERTS - 2), jnp.bfloat16),
        ],
        axis=1,
    )
    first_full = lax.all_gather(first_pack, "fsdp", axis=0, tiled=True)
    qkv_width = MODEL_WIDTH + 2 * kv_width
    query_full = first_full[:, :MODEL_WIDTH]
    key_full = first_full[:, MODEL_WIDTH : MODEL_WIDTH + kv_width]
    value_full = first_full[:, MODEL_WIDTH + kv_width : qkv_width]
    qkv_full = first_full[:, :qkv_width]
    router_full = first_full[:, qkv_width : qkv_width + EXPERTS]
    attn_gain = first_full[:, qkv_width + EXPERTS]
    moe_gain = first_full[:, qkv_width + EXPERTS + 1]
    outproj_full = lax.all_gather(out_weight, "fsdp", axis=0, tiled=True)
    grad_all = ring_gather(out_grad, n_expert)
    routes_all = lax.all_gather(routes, "expert", axis=0, tiled=False)
    x_float = tokens.astype(jnp.float32)
    gain_first = attn_gain.astype(jnp.float32)
    normed_one, norm_one_back = jax.vjp(rms_scale, x_float, gain_first)
    normed_low = normed_one.astype(jnp.bfloat16)
    query_pre = jnp.dot(normed_low, query_full, preferred_element_type=jnp.float32)
    key_before_rotation = jnp.dot(normed_low, key_full, preferred_element_type=jnp.float32)
    value_reduced = jnp.dot(normed_low, value_full, preferred_element_type=jnp.float32).astype(
        jnp.bfloat16
    )
    cosine_table, sine_table = rope_tables(token_rows, HEAD_WIDTH)
    query_rotated = apply_rotation_heads(
        query_pre.reshape(token_rows, QUERY_HEADS, HEAD_WIDTH), cosine_table, sine_table, 1.0
    ).astype(jnp.bfloat16)
    query_rotated = query_rotated.reshape(
        token_rows, KEY_VALUE_HEADS, query_group_width, HEAD_WIDTH
    )
    key_rotated = apply_rotation_heads(
        key_before_rotation.reshape(token_rows, KEY_VALUE_HEADS, HEAD_WIDTH),
        cosine_table,
        sine_table,
        1.0,
    ).astype(jnp.bfloat16)
    value_per_head = value_reduced.reshape(token_rows, KEY_VALUE_HEADS, HEAD_WIDTH)
    masked = masked_scores(query_rotated, key_rotated)
    row_top = jnp.max(masked, axis=-1, keepdims=True)
    expo = jnp.exp(masked - row_top)
    row_total = jnp.sum(expo, axis=-1, keepdims=True)
    log_total = row_top + jnp.log(row_total)
    probability_reduced = (expo / row_total).astype(jnp.bfloat16)
    attn_heads = jnp.einsum(
        "nfea,anm->enfm", probability_reduced, value_per_head, preferred_element_type=jnp.float32
    )
    attn_low = attn_heads.reshape(token_rows, QUERY_HEADS * HEAD_WIDTH).astype(jnp.bfloat16)
    attn_proj = jnp.dot(attn_low, outproj_full, preferred_element_type=jnp.float32)
    resid_one = x_float + attn_proj
    gain_second = moe_gain.astype(jnp.float32)
    normed_two, norm_two_back = jax.vjp(rms_scale, resid_one, gain_second)
    moe_input = normed_two.astype(jnp.bfloat16)
    moe_all = lax.all_gather(moe_input, "expert", axis=0, tiled=False)
    gates = dense_gates(moe_input, router_full, routes)
    first_expert = lax.axis_index("expert") * exp_local
    own_ids = first_expert + jnp.arange(exp_local)
    own_mask = jnp.any(routes_all[:, :, :, None] == own_ids, axis=2)
    earlier = (jnp.arange(token_rows)[:, None] > jnp.arange(token_rows)[None, :]).astype(
        jnp.bfloat16
    )
    slots = jnp.einsum(
        "tu,nue->net", earlier, own_mask.astype(jnp.bfloat16), preferred_element_type=jnp.float32
    )
    slots = jnp.where(jnp.swapaxes(own_mask, 1, 2), slots, -1.0).astype(jnp.int32)
    hit = slots[:, :, None, :] == jnp.arange(CAP)[None, None, :, None]
    place = hit.astype(jnp.bfloat16)
    grad_rows = jnp.einsum(
        "nest,ntd->nesd", place, grad_all, preferred_element_type=jnp.float32
    ).astype(jnp.bfloat16)
    gates_all = dense_gates(moe_all, router_full, routes_all)
    gates_own = lax.dynamic_slice_in_dim(gates_all, first_expert, exp_local, axis=2)
    gate_slot = jnp.sum(
        jnp.where(hit, jnp.swapaxes(gates_own, 1, 2)[:, :, None, :], 0.0), axis=-1, keepdims=True
    )
    arrived_rows = jnp.einsum(
        "nest,ntd->nesd", place, moe_all, preferred_element_type=jnp.float32
    ).astype(jnp.bfloat16)
    gate_part = jnp.einsum(
        "nesd,edf->nesf", arrived_rows, gate_weight, preferred_element_type=jnp.float32
    )
    up_part = jnp.einsum(
        "nesd,edf->nesf", arrived_rows, up_weight, preferred_element_type=jnp.float32
    )
    sigma = jax.nn.sigmoid(gate_part)
    silu_value = gate_part * sigma
    hidden = silu_value * up_part
    hidden_scaled = (gate_slot * hidden).astype(jnp.bfloat16)
    expert_out = jnp.einsum(
        "nesf,efd->nesd", hidden_scaled, down_weight, preferred_element_type=jnp.float32
    ).astype(jnp.bfloat16)
    out_home = jnp.einsum(
        "nest,nesd->ntd", place, expert_out, preferred_element_type=jnp.float32
    ).astype(jnp.bfloat16)
    out_home, grad_rows = lax.optimization_barrier((out_home, grad_rows))
    moe_sum = lax.psum_scatter(out_home, "expert", scatter_dimension=0, tiled=False)
    down_local = jnp.einsum(
        "nesf,nesd->efd", hidden_scaled, grad_rows, preferred_element_type=jnp.float32
    )
    hidden_back = jnp.einsum(
        "nesd,efd->nesf", grad_rows, down_weight, preferred_element_type=jnp.float32
    )
    score_slot = jnp.sum(hidden * hidden_back, axis=-1)
    score_token = jnp.sum(jnp.where(hit, score_slot[:, :, :, None], 0.0), axis=2)
    gate_score = lax.all_to_all(score_token, "expert", split_axis=0, concat_axis=0, tiled=True)
    gate_score = gate_score.reshape(EXPERTS, token_rows).T
    hidden_grad = gate_slot * hidden_back
    gate_low = (hidden_grad * up_part * sigma * (1.0 + gate_part * (1.0 - sigma))).astype(
        jnp.bfloat16
    )
    up_low = (hidden_grad * silu_value).astype(jnp.bfloat16)
    row_grad = jnp.einsum(
        "nesf,edf->nesd", gate_low, gate_weight, preferred_element_type=jnp.float32
    )
    row_grad = (
        row_grad
        + jnp.einsum("nesf,edf->nesd", up_low, up_weight, preferred_element_type=jnp.float32)
    ).astype(jnp.bfloat16)
    row_home = jnp.einsum(
        "nest,nesd->ntd", place, row_grad, preferred_element_type=jnp.float32
    ).astype(jnp.bfloat16)
    row_sum = lax.psum_scatter(row_home, "expert", scatter_dimension=0, tiled=False)
    block_out = (resid_one + moe_sum.astype(jnp.float32)).astype(jnp.bfloat16)
    gate_local = jnp.einsum(
        "nesd,nesf->edf", arrived_rows, gate_low, preferred_element_type=jnp.float32
    )
    up_local = jnp.einsum(
        "nesd,nesf->edf", arrived_rows, up_low, preferred_element_type=jnp.float32
    )
    down_low = down_local.astype(jnp.bfloat16)
    gate_grad_low = gate_local.astype(jnp.bfloat16)
    up_grad_low = up_local.astype(jnp.bfloat16)
    down_sum = fsdp_sum(down_low)
    gate_sum = fsdp_sum(gate_grad_low)
    up_sum = fsdp_sum(up_grad_low)
    row_sum, _, _, _ = lax.optimization_barrier(
        (row_sum, down_low, gate_grad_low, up_grad_low)
    )
    grad_float = out_grad.astype(jnp.float32)
    logit_grad = gates * (gate_score - jnp.sum(gates * gate_score, axis=-1, keepdims=True))
    router_local = jnp.dot(moe_input.astype(jnp.float32).T, logit_grad, precision=HIGH_PRECISION)
    router_back = jnp.dot(logit_grad, router_full.astype(jnp.float32).T, precision=HIGH_PRECISION)
    normed_two_grad = row_sum.astype(jnp.float32) + router_back
    resid_from_norm, gain_two_grad = norm_two_back(normed_two_grad)
    resid_grad = grad_float + resid_from_norm
    proj_low = resid_grad.astype(jnp.bfloat16)
    outproj_local = inner_rows(attn_low, proj_low)
    early = reduce_pack([outproj_local, router_local, gain_two_grad[:, None]], n_expert)
    head_outputs_gradient = (
        outer_cols(proj_low, outproj_full)
        .astype(jnp.bfloat16)
        .reshape(token_rows, KEY_VALUE_HEADS, query_group_width, HEAD_WIDTH)
    )
    attention_probability = jnp.exp(masked_scores(query_rotated, key_rotated) - log_total)
    probability_recomputed = attention_probability.astype(jnp.bfloat16)
    value_reduced_gradient = jnp.einsum(
        "jfek,ejfa->kja",
        probability_recomputed,
        head_outputs_gradient,
        preferred_element_type=jnp.float32,
    )
    value_reduced_gradient = value_reduced_gradient.reshape(
        token_rows, KEY_VALUE_HEADS * HEAD_WIDTH
    ).astype(jnp.bfloat16)
    prob_grad = jnp.einsum(
        "mhwo,pho->hwmp", head_outputs_gradient, value_per_head, preferred_element_type=jnp.float32
    )
    scores_gradient = (
        attention_probability
        * (prob_grad - jnp.sum(attention_probability * prob_grad, axis=-1, keepdims=True))
    ).astype(jnp.bfloat16)
    query_rot_grad = jnp.einsum(
        "nfea,anm->enfm", scores_gradient, key_rotated, preferred_element_type=jnp.float32
    ) * HEAD_WIDTH ** (-0.5)
    key_rot_grad = jnp.einsum(
        "jfek,ejfa->kja", scores_gradient, query_rotated, preferred_element_type=jnp.float32
    ) * HEAD_WIDTH ** (-0.5)
    query_low_grad = (
        apply_rotation_heads(
            query_rot_grad.reshape(token_rows, QUERY_HEADS, HEAD_WIDTH),
            cosine_table,
            sine_table,
            -1.0,
        )
        .reshape(token_rows, QUERY_HEADS * HEAD_WIDTH)
        .astype(jnp.bfloat16)
    )
    key_low_grad = (
        apply_rotation_heads(key_rot_grad, cosine_table, sine_table, -1.0)
        .reshape(token_rows, KEY_VALUE_HEADS * HEAD_WIDTH)
        .astype(jnp.bfloat16)
    )
    query_local = inner_rows(normed_low, query_low_grad)
    key_local = inner_rows(normed_low, key_low_grad)
    value_local = inner_rows(normed_low, value_reduced_gradient)
    normed_one_grad = (
        outer_cols(query_low_grad, query_full)
        + outer_cols(key_low_grad, key_full)
        + outer_cols(value_reduced_gradient, value_full)
    )
    x_from_norm, gain_one_grad = norm_one_back(normed_one_grad)
    input_grad = resid_grad + x_from_norm
    late = reduce_pack(
        [query_local, key_local, value_local, gain_one_grad[:, None]], n_expert
    )
    query_c = late[:, :MODEL_WIDTH]
    key_c = late[:, MODEL_WIDTH : MODEL_WIDTH + kv_width]
    value_c = late[:, MODEL_WIDTH + kv_width : qkv_width]
    gain_c = late[:, qkv_width]
    outproj_c = early[:, :MODEL_WIDTH]
    router_c = early[:, MODEL_WIDTH : MODEL_WIDTH + EXPERTS]
    gain_d = early[:, MODEL_WIDTH + EXPERTS]
    return (
        block_out,
        input_grad,
        gain_c,
        query_c,
        key_c,
        value_c,
        outproj_c,
        gain_d,
        router_c,
        gate_sum,
        up_sum,
        down_sum,
    )


def solution(mesh):
    return jax.shard_map(
        on_device,
        mesh=mesh,
        in_specs=(
            P(("expert", "fsdp"), None),
            P("fsdp"),
            P("fsdp", None),
            P("fsdp", None),
            P("fsdp", None),
            P("fsdp", None),
            P("fsdp"),
            P("fsdp", None),
            P("expert", None, None),
            P("expert", None, None),
            P("expert", None, None),
            P(("expert", "fsdp"), None),
            P(("expert", "fsdp"), None),
        ),
        out_specs=(
            P(("expert", "fsdp"), None),
            P(("expert", "fsdp"), None),
            P("fsdp"),
            P("fsdp", None),
            P("fsdp", None),
            P("fsdp", None),
            P("fsdp", None),
            P("fsdp"),
            P("fsdp", None),
            P("expert", None, None),
            P("expert", None, None),
            P("expert", None, None),
        ),
        check_vma=False,
    )
```
